32 devices in a mesh: dp: 8 (over y, x, core), ctx: 4 (over z).
Axes of the slice: x: 2, y: 2, z: 4, core: 2. Of those that a mesh axis runs over, the one named last changes fastest.
Arguments:
- tokens: bfloat16 [32, 512, 1024], P('dp', 'ctx'), may hold values from -6 to 6
- cotangent: bfloat16 [32, 512, 1024], P('dp', 'ctx'), may hold values from -6 to 6
- counts: int32 [8], P('dp'), may hold values from 1 to 4, as said below
- block_order: int32 [32, 4], P('dp'), may hold values from 0 to 3, each once within a row
- qkv_weight: float32 [1024, 3072], P(('dp', 'ctx')), may hold values from -0.25 to 0.25
- qkv_first: float32 [1024, 3072], P(('dp', 'ctx')), may hold values from -64 to 64
- qkv_second: float32 [1024, 3072], P(('dp', 'ctx')), may hold values from 557.056 to 2211.84
- proj_weight: float32 [1024, 1024], P(('dp', 'ctx')), may hold values from -1 to 1
- proj_first: float32 [1024, 1024], P(('dp', 'ctx')), may hold values from -10 to 10
- proj_second: float32 [1024, 1024], P(('dp', 'ctx')), may hold values from 14.7456 to 58.9824
- up_weight: float32 [1024, 4096], P(('dp', 'ctx')), may hold values from -0.1875 to 0.1875
- up_first: float32 [1024, 4096], P(('dp', 'ctx')), may hold values from -20 to 20
- up_second: float32 [1024, 4096], P(('dp', 'ctx')), may hold values from 45.8752 to 181.8624
- down_weight: float32 [4096, 1024], P(('dp', 'ctx')), may hold values from -0.09375 to 0.09375
- down_first: float32 [4096, 1024], P(('dp', 'ctx')), may hold values from -40 to 40
- down_second: float32 [4096, 1024], P(('dp', 'ctx')), may hold values from 175.3088 to 697.9584
- vectors: float32 [12, 1024], P(None, ('dp', 'ctx')), may hold values from -1.5 to 1.5, as said below
- vectors_first: float32 [12, 1024], P(None, ('dp', 'ctx')), may hold values from -80 to 80
- vectors_second: float32 [12, 1024], P(None, ('dp', 'ctx')), may hold values from 861.7984 to 3440.64
Outputs:
- layer_out: bfloat16 [32, 512, 1024], P('dp', 'ctx')
- token_grad: float32 [32, 512, 1024], P('dp', 'ctx')
- qkv_new: float32 [1024, 3072], P(('dp', 'ctx'))
- qkv_mean: float32 [1024, 3072], P(('dp', 'ctx'))
- qkv_square: float32 [1024, 3072], P(('dp', 'ctx'))
- proj_new: float32 [1024, 1024], P(('dp', 'ctx'))
- proj_mean: float32 [1024, 1024], P(('dp', 'ctx'))
- proj_square: float32 [1024, 1024], P(('dp', 'ctx'))
- up_new: float32 [1024, 4096], P(('dp', 'ctx'))
- up_mean: float32 [1024, 4096], P(('dp', 'ctx'))
- up_square: float32 [1024, 4096], P(('dp', 'ctx'))
- down_new: float32 [4096, 1024], P(('dp', 'ctx'))
- down_mean: float32 [4096, 1024], P(('dp', 'ctx'))
- down_square: float32 [4096, 1024], P(('dp', 'ctx'))
- vectors_new: float32 [12, 1024], P(None, ('dp', 'ctx'))
- vectors_mean: float32 [12, 1024], P(None, ('dp', 'ctx'))
- vectors_square: float32 [12, 1024], P(None, ('dp', 'ctx'))
The draws below stay inside these ranges and needn't reach their ends.
Inputs may be any that keep to these rules, and one draw needn't show every extreme that they name: Some group holds 4 live sequences; slot s is live where s % 4 < counts[s // 4]. Each row is a permutation: ctx device c holds the positions block_order[s, c] * 128 to block_order[s, c] * 128 + 127 of sequence s. `vectors`: rows 0 and 5 are the norms' gains, the other rows biases.
All inputs are finite; a program needn't handle non-finite values.
Results may differ from the reference program's by a relative error of at most 0.013.
The reference program's roundings to bfloat16 on the way count: a program that leaves them out, or rounds other values in their place, can miss the bound.
Values may be sent and summed in bfloat16 or wider, within the bound.
A program may use at most 192 MiB of HBM per device.

```python
import math
import jax
import jax.numpy as jnp
from jax import lax

D = 1024
HEAD_DIM = 64
FF = 4096
SEQ = 512
SLOTS = 4
STEP = 10
SEQS = 32
NVEC = 12
N_DP = 8
N_CTX = 4


def draw_counts(key, part):
    key = jax.random.fold_in(key, 3)
    first_key, second_key = jax.random.split(key)
    drawn = jax.random.randint(first_key, (N_DP,), 1, SLOTS + 1)
    full = jax.random.randint(second_key, (), 0, N_DP)
    return jnp.where(jnp.arange(N_DP) == full, SLOTS, drawn).astype(jnp.int32)


def draw_vectors(key, part):
    key = jax.random.fold_in(key, 11)
    gain_key, bias_key = jax.random.split(key)
    gains = jax.random.uniform(gain_key, (NVEC, D), jnp.float32, 0.5, 1.5)
    biases = jnp.clip(0.3 * jax.random.normal(bias_key, (NVEC, D), jnp.float32), -1.5, 1.5)
    row = jnp.arange(NVEC)[:, None]
    return jnp.where((row == 0) | (row == 5), gains, biases).astype(jnp.float32)


def steps_of(stream_key, shape, cuts, smallest, largest):
    def one(position, parts):
        heights = jax.random.uniform(jax.random.fold_in(jax.random.fold_in(stream_key, 6), position), (parts,), jnp.float32, smallest / len(cuts), largest / len(cuts))
        return jnp.repeat(jnp.exp(heights), shape[position] // parts).reshape((-1,) + (1,) * (len(shape) - position - 1))

    loudness = one(*cuts[0])
    for cut in cuts[1:]:
        loudness = loudness * one(*cut)
    return loudness


def scatter_about(stream_key, extent, scale, most, pieces=(), held_as=jnp.bfloat16):
    level = steps_of(stream_key, extent, pieces, -0.22, 0.18) if pieces else 1.0
    values = jax.random.normal(stream_key, extent, jnp.float32) * scale * level
    return jnp.minimum(jnp.maximum(values, -most), most).astype(held_as)


def setup_inputs(seed: int = 0) -> dict:
    streams_of = jax.random.split(jax.random.key(seed), 20)
    return {
        "tokens": scatter_about(streams_of[0], (SEQS, SEQ, D), 1.0, 6.0, ((0, 8), (1, 4))),
        "cotangent": scatter_about(streams_of[1], (SEQS, SEQ, D), 1.0, 6.0, ((0, 8), (1, 4))),
        "counts": draw_counts(jax.random.fold_in(streams_of[19], 71), 0),
        "block_order": jax.vmap(lambda own: jax.random.permutation(own, N_CTX))(jax.random.split(streams_of[3], SEQS)).reshape((SEQS, N_CTX)).astype(jnp.int32),
        "qkv_weight": scatter_about(streams_of[4], (D, 3 * D), (D // 2) ** -0.5, 0.25, ((0, 32),), jnp.float32),
        "qkv_first": scatter_about(streams_of[5], (D, 3 * D), (0.089 * (SLOTS * N_DP * SEQ) ** 0.5), 64.0, ((0, 32),), jnp.float32),
        "qkv_second": jnp.clip(jnp.exp(math.log(2211.84) - 1.3789142 * jax.random.uniform(streams_of[6], (D, 3 * D), jnp.float32) ** steps_of(streams_of[6], (D, 3 * D), ((0, 32),), -0.2, 0.2)), 557.056, 2211.84),
        "proj_weight": scatter_about(streams_of[7], (D, D), (D // 32) ** -0.5, 1.0, ((0, 32),), jnp.float32),
        "proj_first": scatter_about(streams_of[8], (D, D), (0.0144 * (SLOTS * N_DP * SEQ) ** 0.5), 10.0, ((0, 32),), jnp.float32),
        "proj_second": jnp.clip(jnp.exp(math.log(58.9824) - 1.3862944 * jax.random.uniform(streams_of[9], (D, D), jnp.float32) ** steps_of(streams_of[9], (D, D), ((0, 32),), -0.2, 0.2)), 14.7456, 58.9824),
        "up_weight": scatter_about(streams_of[10], (D, FF), D ** -0.5, 0.1875, ((0, 32),), jnp.float32),
        "up_first": scatter_about(streams_of[11], (D, FF), (0.0255 * (SLOTS * N_DP * SEQ) ** 0.5), 20.0, ((0, 32),), jnp.float32),
        "up_second": jnp.clip(jnp.exp(math.log(181.8624) - 1.3773257 * jax.random.uniform(streams_of[12], (D, FF), jnp.float32) ** steps_of(streams_of[12], (D, FF), ((0, 32),), -0.2, 0.2)), 45.8752, 181.8624),
        "down_weight": scatter_about(streams_of[13], (FF, D), FF ** -0.5, 0.09375, ((0, 32),), jnp.float32),
        "down_first": scatter_about(streams_of[14], (FF, D), (0.05 * (SLOTS * N_DP * SEQ) ** 0.5), 40.0, ((0, 32),), jnp.float32),
        "down_second": jnp.clip(jnp.exp(math.log(697.9584) - 1.3816104 * jax.random.uniform(streams_of[15], (FF, D), jnp.float32) ** steps_of(streams_of[15], (FF, D), ((0, 32),), -0.2, 0.2)), 175.3088, 697.9584),
        "vectors": draw_vectors(jax.random.fold_in(streams_of[19], 71), 0),
        "vectors_first": scatter_about(streams_of[17], (NVEC, D), (0.111 * (SLOTS * N_DP * SEQ) ** 0.5), 80.0, ((1, 32),), jnp.float32),
        "vectors_second": jnp.clip(jnp.exp(math.log(3440.64) - 1.3843914 * jax.random.uniform(streams_of[18], (NVEC, D), jnp.float32) ** steps_of(streams_of[18], (NVEC, D), ((1, 32),), -0.2, 0.2)), 861.7984, 3440.64),
    }


@jax.custom_vjp
def low(v):
    return lax.optimization_barrier(v.astype(jnp.bfloat16)).astype(jnp.float32)

@jax.custom_vjp
def low_back(v):
    return v

def low_keep(v):
    return (low(v), None)

def low_pass(kept, grad):
    return (grad,)

def back_keep(v):
    return (v, None)

def back_low(kept, grad):
    return (low(grad),)
low.defvjp(low_keep, low_pass)
low_back.defvjp(back_keep, back_low)
beta_one = 0.9
beta_two = 0.95
epsilon = 1e-08
weight_decay = 0.1
rate_matrix = 0.1
rate_output = 0.5
rate_vector = 0.4
norm_eps = 1e-05

def layer_norm(values, gain, shift):
    center = values - lax.optimization_barrier(jnp.mean(values, -1, keepdims=True))
    variance = lax.optimization_barrier(jnp.mean(center * center, -1, keepdims=True))
    return center * lax.rsqrt(variance + norm_eps) * gain + shift

def gelu_tanh(values):
    return 0.5 * values * (1.0 + jnp.tanh(0.7978845608 * (values + 0.044715 * values * values * values)))

def product(left, right):
    return jnp.matmul(left, right, precision=lax.Precision.HIGHEST)

def both_ways(values):
    return low(low_back(values))

def forward(tokens, qkv_w, proj_w, up_w, down_w, table, positions, live):
    qkv_w = low(qkv_w)
    proj_w = low(proj_w)
    up_w = low(up_w)
    down_w = low(down_w)
    table = low(table)
    count, length, width = tokens.shape
    heads = width // HEAD_DIM
    up_bias = table[8:].reshape(-1)
    normed = low(layer_norm(tokens, table[0], table[1]))
    mixed = product(normed, qkv_w)
    queries = both_ways(mixed[..., :width] + table[2]).reshape(count, length, heads, HEAD_DIM)
    keys = both_ways(mixed[..., width:2 * width]).reshape(count, length, heads, HEAD_DIM)
    values = both_ways(mixed[..., 2 * width:] + table[3]).reshape(count, length, heads, HEAD_DIM)
    scores = low_back(jnp.einsum('gqhd,gkhd->ghqk', queries, keys, precision=lax.Precision.HIGHEST) * HEAD_DIM ** (-0.5))
    allowed = positions[:, None, None, :] <= positions[:, None, :, None]
    scores = jnp.where(allowed, scores, -1e+30)
    top = lax.optimization_barrier(jnp.max(scores, -1, keepdims=True))
    expd = jnp.exp(scores - top)
    attention = low(expd / lax.optimization_barrier(jnp.sum(expd, -1, keepdims=True)))
    attended = both_ways(jnp.einsum('ghqk,gkhd->gqhd', attention, values, precision=lax.Precision.HIGHEST).reshape(count, length, width))
    middle = tokens + low_back(product(attended, proj_w) + table[4])
    normed2 = low(layer_norm(middle, table[5], table[6]))
    hidden = low_back(product(normed2, up_w) + up_bias)
    active = low(gelu_tanh(hidden))
    result = middle + product(active, down_w) + table[7]
    return result * live[:, None, None]

def adam_update(weight, first, second, grad, rate, decay_now):
    first_new = beta_one * first + (1.0 - beta_one) * grad
    second_new = beta_two * second + (1.0 - beta_two) * grad * grad
    step_size = first_new / (1.0 - beta_one ** STEP) / (jnp.sqrt(second_new / (1.0 - beta_two ** STEP)) + epsilon)
    return (weight - rate * (step_size + decay_now * weight), first_new, second_new)

def reference(tokens, cotangent, counts, block_order, qkv_weight, qkv_first, qkv_second, proj_weight, proj_first, proj_second, up_weight, up_first, up_second, down_weight, down_first, down_second, vectors, vectors_first, vectors_second):
    span = SEQ // N_CTX
    rows = jnp.arange(SEQ, dtype=jnp.int32)
    positions = (block_order[:, rows // span] * span + rows % span).astype(jnp.int32)
    index = jnp.arange(SEQS, dtype=jnp.int32)
    live = jnp.where(index % SLOTS < counts[index // SLOTS], 1.0, 0.0).astype(jnp.float32)

    def one_group(totals, block):
        group_tokens, group_cot, group_pos, group_live = block

        def run(inputs, qkv_w, proj_w, up_w, down_w, table):
            return forward(inputs, qkv_w, proj_w, up_w, down_w, table, group_pos, group_live)
        result, pull = jax.vjp(run, group_tokens.astype(jnp.float32), qkv_weight, proj_weight, up_weight, down_weight, vectors)
        grads = pull(group_cot.astype(jnp.float32))
        totals = tuple((total + grad for total, grad in zip(totals, grads[1:])))
        return (totals, (result.astype(jnp.bfloat16), grads[0]))
    start = (jnp.zeros_like(qkv_weight), jnp.zeros_like(proj_weight), jnp.zeros_like(up_weight), jnp.zeros_like(down_weight), jnp.zeros_like(vectors))
    blocks = (tokens.reshape(N_DP, SLOTS, SEQ, D), cotangent.reshape(N_DP, SLOTS, SEQ, D), positions.reshape(N_DP, SLOTS, SEQ), live.reshape(N_DP, SLOTS))
    totals, stacked = lax.scan(one_group, start, blocks)
    layer_out = stacked[0].reshape(SEQS, SEQ, D)
    token_grad = stacked[1].reshape(SEQS, SEQ, D)
    qkv_new, qkv_mean, qkv_square = adam_update(qkv_weight, qkv_first, qkv_second, totals[0], rate_matrix, weight_decay)
    proj_new, proj_mean, proj_square = adam_update(proj_weight, proj_first, proj_second, totals[1], rate_output, weight_decay)
    up_new, up_mean, up_square = adam_update(up_weight, up_first, up_second, totals[2], rate_matrix, weight_decay)
    down_new, down_mean, down_square = adam_update(down_weight, down_first, down_second, totals[3], rate_matrix, weight_decay)
    vectors_new, vectors_mean, vectors_square = adam_update(vectors, vectors_first, vectors_second, totals[4], rate_vector, 0.0)
    return (layer_out, token_grad, qkv_new, qkv_mean, qkv_square, proj_new, proj_mean, proj_square, up_new, up_mean, up_square, down_new, down_mean, down_square, vectors_new, vectors_mean, vectors_square)
```

```python
import jax
import jax.numpy as jnp
from jax import lax
from jax.experimental import pallas as pl
from jax.experimental.pallas import tpu as pltpu
from jax.sharding import PartitionSpec as P

HEAD_DIM = 64
STEP = 10


beta_one = 0.9
beta_two = 0.95
epsilon = 1e-08
weight_decay = 0.1
rate_matrix = 0.1
rate_output = 0.5
rate_vector = 0.4
norm_eps = 1e-05


def layer_norm(values, gain, shift):
    center = values - jnp.mean(values, -1, keepdims=True)
    variance = jnp.mean(center * center, -1, keepdims=True)
    return center * lax.rsqrt(variance + norm_eps) * gain + shift


def gelu_tanh(values):
    return (
        0.5
        * values
        * (1.0 + jnp.tanh(0.7978845608 * (values + 0.044715 * values * values * values)))
    )


def adam_update(weight, first, second, grad, rate, decay_now):
    first_new = beta_one * first + (1.0 - beta_one) * grad
    second_new = beta_two * second + (1.0 - beta_two) * grad * grad
    step_size = (
        first_new
        / (1.0 - beta_one**STEP)
        / (jnp.sqrt(second_new / (1.0 - beta_two**STEP)) + epsilon)
    )
    return (weight - rate * (step_size + decay_now * weight), first_new, second_new)


def levels():
    return lax.axis_size("dp").bit_length() - 1


def own_bit(bit):
    return (lax.axis_index("dp") // 2**bit) % 2


def swap(array, bit):
    return lax.ppermute(array, "dp", [(d, d ^ (1 << bit)) for d in range(lax.axis_size("dp"))])


def shift(array, by):
    n = lax.axis_size("ctx")
    return lax.ppermute(array, "ctx", [(c, (c + by) % n) for c in range(n)])


def pick(array, index, axis=0):
    return lax.dynamic_index_in_dim(array, index, axis, keepdims=False)


def put(array, piece, index, axis=0):
    return lax.dynamic_update_index_in_dim(array, piece, index, axis)


def to_sequence(array, order):
    n = lax.axis_size("ctx")
    me = lax.axis_index("ctx")
    out = jnp.zeros_like(array)
    out = put(out, pick(array, me), order[me])
    for by in range(1, n):
        got = shift(pick(array, (me + by) % n), by)
        out = put(out, got, order[(me - by) % n])
    return out.reshape(-1, array.shape[-1])


def from_sequence(array, order, slots):
    n = lax.axis_size("ctx")
    me = lax.axis_index("ctx")
    blocks = array.reshape(slots, -1, array.shape[-1])
    out = put(jnp.zeros_like(blocks), pick(blocks, order[me]), me)
    for by in range(1, n):
        got = shift(pick(blocks, order[(me + by) % n]), by)
        out = put(out, got, (me - by) % n)
    return out


def gather_rows(shard):
    rows, columns = shard.shape
    n = lax.axis_size("ctx")
    me = lax.axis_index("ctx")
    k = levels()
    whole = put(jnp.zeros((n, rows, columns), shard.dtype), shard, me)
    for by in range(1, n):
        whole = put(whole, shift(shard, by), (me - by) % n)
    bits = list(range(1, k))
    cut = columns // 256 * 128
    halves = []
    for order, part in ((bits, whole[:, :, :cut]), (bits[::-1], whole[:, :, cut:])):
        done = []
        for bit in order:
            axis = sum(1 for other in done if other > bit)
            got = swap(part, bit)
            done.append(bit)
            shape = part.shape[:axis] + (2,) + part.shape[axis:]
            part = put(put(jnp.zeros(shape, part.dtype), part, own_bit(bit), axis), got, 1 - own_bit(bit), axis)
        halves.append(part)
    mine = jnp.concatenate(halves, -1)
    got = swap(mine, 0)
    axis = k - 1
    shape = mine.shape[:axis] + (2,) + mine.shape[axis:]
    full = put(put(jnp.zeros(shape, mine.dtype), mine, own_bit(0), axis), got, 1 - own_bit(0), axis)
    return full.reshape(-1, columns)


def scatter_product(left, right):
    count, rows = left.shape
    columns = right.shape[1]
    n = lax.axis_size("ctx")
    me = lax.axis_index("ctx")
    k = levels()
    groups = 2 ** (k - 1)
    each = rows // (2 * groups)
    split = left.reshape(count, groups, 2, each)

    def half(index):
        part = pick(split, index, 2).reshape(count, groups * each)
        return jnp.einsum("rd,re->de", part, right, preferred_element_type=jnp.float32)

    got = swap(half(1 - own_bit(0)).astype(jnp.bfloat16), 0)
    total = (half(own_bit(0)) + got.astype(jnp.float32)).astype(jnp.bfloat16)
    total = total.reshape((2,) * (k - 1) + (n, each // n, columns))
    bits = list(range(1, k))
    cut = columns // 256 * 128
    halves = []
    for order, part in ((bits, total[..., :cut]), (bits[::-1], total[..., cut:])):
        left_bits = sorted(bits, reverse=True)
        for bit in order:
            axis = left_bits.index(bit)
            got = swap(pick(part, 1 - own_bit(bit), axis), bit)
            part = (pick(part, own_bit(bit), axis).astype(jnp.float32) + got.astype(jnp.float32)).astype(jnp.bfloat16)
            left_bits.remove(bit)
        halves.append(part)
    part = jnp.concatenate(halves, -1)
    out = pick(part, me).astype(jnp.float32)
    for by in range(1, n):
        out = out + shift(pick(part, (me + by) % n), by).astype(jnp.float32)
    return out


def probabilities(queries, keys, first):
    scores = lax.dot_general(
        queries, keys, (((1,), (1,)), ((), ())), preferred_element_type=jnp.float32
    ) * (HEAD_DIM ** (-0.5))
    row = lax.broadcasted_iota(jnp.int32, scores.shape, 0) + first
    column = lax.broadcasted_iota(jnp.int32, scores.shape, 1)
    scores = jnp.where(column <= row, scores, -1e30)
    expd = jnp.exp(scores - jnp.max(scores, -1, keepdims=True))
    return expd / jnp.sum(expd, -1, keepdims=True)


def attend_kernel(q_ref, k_ref, v_ref, o_ref):
    length = q_ref.shape[0]
    step = length // 2
    outs = []
    for head in range(q_ref.shape[1] // HEAD_DIM):
        lanes = slice(head * HEAD_DIM, (head + 1) * HEAD_DIM)
        parts = []
        for first in range(0, length, step):
            last = first + step
            p = probabilities(q_ref[first:last, lanes], k_ref[:last, lanes], first)
            parts.append(
                jnp.dot(p.astype(jnp.bfloat16), v_ref[:last, lanes], preferred_element_type=jnp.float32)
            )
        outs.append(jnp.concatenate(parts, 0))
    o_ref[...] = jnp.concatenate(outs, 1).astype(o_ref.dtype)


def attend_back_kernel(q_ref, k_ref, v_ref, g_ref, dq_ref, dk_ref, dv_ref):
    length = q_ref.shape[0]
    step = length // 2
    scale = HEAD_DIM ** (-0.5)
    all_q, all_k, all_v = [], [], []
    for head in range(q_ref.shape[1] // HEAD_DIM):
        lanes = slice(head * HEAD_DIM, (head + 1) * HEAD_DIM)
        dqs, dks, dvs = [], [], []
        for first in range(0, length, step):
            last = first + step
            q, g = q_ref[first:last, lanes], g_ref[first:last, lanes]
            k, v = k_ref[:last, lanes], v_ref[:last, lanes]
            p = probabilities(q, k, first)
            dp = lax.dot_general(g, v, (((1,), (1,)), ((), ())), preferred_element_type=jnp.float32)
            ds = (p * (dp - jnp.sum(p * dp, -1, keepdims=True))).astype(jnp.bfloat16)
            low = p.astype(jnp.bfloat16)
            dqs.append(jnp.dot(ds, k, preferred_element_type=jnp.float32) * scale)
            dks.append(
                lax.dot_general(ds, q, (((0,), (0,)), ((), ())), preferred_element_type=jnp.float32)
            )
            dvs.append(
                lax.dot_general(low, g, (((0,), (0,)), ((), ())), preferred_element_type=jnp.float32)
            )
        all_q.append(jnp.concatenate(dqs, 0))
        all_k.append(jnp.concatenate((dks[0] + dks[1][:step], dks[1][step:]), 0) * scale)
        all_v.append(jnp.concatenate((dvs[0] + dvs[1][:step], dvs[1][step:]), 0))
    dq_ref[...] = jnp.concatenate(all_q, 1).astype(dq_ref.dtype)
    dk_ref[...] = jnp.concatenate(all_k, 1).astype(dk_ref.dtype)
    dv_ref[...] = jnp.concatenate(all_v, 1).astype(dv_ref.dtype)


def attend(mixed):
    length, columns = mixed.shape
    width = columns // 3
    pairs = width // 128

    def block(which):
        return pl.BlockSpec((length, 128), lambda h: (0, which * pairs + h))

    return pl.pallas_call(
        attend_kernel,
        grid=(pairs,),
        in_specs=[block(0), block(1), block(2)],
        out_specs=block(0),
        out_shape=jax.ShapeDtypeStruct((length, width), jnp.bfloat16),
        compiler_params=pltpu.CompilerParams(vmem_limit_bytes=48 * 2**20),
        cost_estimate=pl.CostEstimate(
            flops=4 * length * length * width, bytes_accessed=8 * length * width, transcendentals=0
        ),
    )(mixed, mixed, mixed)


def attend_back(mixed, grad):
    length, columns = mixed.shape
    width = columns // 3
    pairs = width // 128

    def block(which):
        return pl.BlockSpec((length, 128), lambda h: (0, which * pairs + h))

    return pl.pallas_call(
        attend_back_kernel,
        grid=(pairs,),
        in_specs=[block(0), block(1), block(2), block(0)],
        out_specs=[block(0)] * 3,
        out_shape=[jax.ShapeDtypeStruct((length, width), jnp.bfloat16)] * 3,
        compiler_params=pltpu.CompilerParams(vmem_limit_bytes=48 * 2**20),
        cost_estimate=pl.CostEstimate(
            flops=10 * length * length * width, bytes_accessed=14 * length * width, transcendentals=0
        ),
    )(mixed, mixed, mixed, grad)


def shards(
    tokens,
    cotangent,
    counts,
    block_order,
    qkv_weight,
    qkv_first,
    qkv_second,
    proj_weight,
    proj_first,
    proj_second,
    up_weight,
    up_first,
    up_second,
    down_weight,
    down_first,
    down_second,
    vectors,
    vectors_first,
    vectors_second,
):
    slots, span, width = tokens.shape
    ranks = lax.axis_size("ctx")
    length = span * ranks
    me = lax.axis_index("ctx")
    pad = 128
    sequence_order = lax.dynamic_index_in_dim(block_order, me, 0, keepdims=False)
    extra = vectors.T.astype(jnp.bfloat16)
    entries = extra.shape[1]
    extra = jnp.pad(extra, ((0, 0), (0, pad - entries)))
    full_qkv = gather_rows(qkv_weight.astype(jnp.bfloat16))
    table_shard = jnp.concatenate((proj_weight.astype(jnp.bfloat16), extra), 1)
    full_ext = gather_rows(table_shard)
    full_up = gather_rows(up_weight.astype(jnp.bfloat16))
    full_down = gather_rows(down_weight.astype(jnp.bfloat16))
    full_proj = full_ext[:, :width]
    table = full_ext[:, width : width + entries].T.astype(jnp.float32)
    up_bias = table[8:].reshape(-1)
    live = jnp.where(me < counts[0], 1.0, 0.0).astype(jnp.float32)
    flat = to_sequence(tokens, sequence_order).astype(jnp.float32)
    grad_out = (to_sequence(cotangent, sequence_order).astype(jnp.float32) * live).astype(jnp.bfloat16)
    normed_full, norm_pull = jax.vjp(layer_norm, flat, table[0], table[1])
    normed = normed_full.astype(jnp.bfloat16)
    bias = jnp.concatenate((table[2], jnp.zeros_like(table[2]), table[3]))
    mixed = (jnp.dot(normed, full_qkv, preferred_element_type=jnp.float32) + bias).astype(jnp.bfloat16)
    attended = attend(mixed)
    middle = flat + jnp.dot(attended, full_proj, preferred_element_type=jnp.float32) + table[4]
    normed2_full, norm2_pull = jax.vjp(layer_norm, middle, table[5], table[6])
    normed2 = normed2_full.astype(jnp.bfloat16)
    hidden = jnp.dot(normed2, full_up, preferred_element_type=jnp.float32) + up_bias
    activated, gelu_pull = jax.vjp(gelu_tanh, hidden)
    active = activated.astype(jnp.bfloat16)
    result = middle + jnp.dot(active, full_down, preferred_element_type=jnp.float32) + table[7]
    layer_out = from_sequence((result * live).astype(jnp.bfloat16), sequence_order, slots)
    down_bias_grad = jnp.sum(grad_out.astype(jnp.float32), 0)
    down_sum = scatter_product(active, grad_out)
    grad_active = jnp.einsum("rd,fd->rf", grad_out, full_down, preferred_element_type=jnp.float32)
    grad_hidden = gelu_pull(grad_active)[0].astype(jnp.bfloat16)
    up_bias_grad = jnp.sum(grad_hidden.astype(jnp.float32), 0)
    up_sum = scatter_product(normed2, grad_hidden)
    grad_normed2 = jnp.einsum("rf,df->rd", grad_hidden, full_up, preferred_element_type=jnp.float32)
    back_middle, gain2_grad, shift2_grad = norm2_pull(grad_normed2)
    grad_middle = grad_out.astype(jnp.float32) + back_middle
    grad_branch = grad_middle.astype(jnp.bfloat16)
    proj_bias_grad = jnp.sum(grad_branch.astype(jnp.float32), 0)
    proj_sum = scatter_product(attended, grad_branch)
    grad_attended = jnp.einsum(
        "re,de->rd", grad_branch, full_proj, preferred_element_type=jnp.float32
    ).astype(jnp.bfloat16)
    grad_queries, grad_keys, grad_values = attend_back(mixed, grad_attended)
    query_bias_grad = jnp.sum(grad_queries.astype(jnp.float32), 0)
    value_bias_grad = jnp.sum(grad_values.astype(jnp.float32), 0)
    grad_mixed = jnp.concatenate((grad_queries, grad_keys, grad_values), -1)
    qkv_sum = scatter_product(normed, grad_mixed)
    grad_normed = jnp.einsum("re,de->rd", grad_mixed, full_qkv, preferred_element_type=jnp.float32)
    back_tokens, gain1_grad, shift1_grad = norm_pull(grad_normed)
    token_grad = from_sequence(
        (grad_middle + back_tokens).astype(jnp.bfloat16), sequence_order, slots
    ).astype(jnp.float32)
    small_grads = jnp.stack(
        (
            gain1_grad,
            shift1_grad,
            query_bias_grad,
            value_bias_grad,
            proj_bias_grad,
            gain2_grad,
            shift2_grad,
            down_bias_grad,
        )
    )
    table_grad = jnp.concatenate((small_grads, up_bias_grad.reshape(-1, width)), 0)
    table_sum = lax.psum_scatter(table_grad, ("dp", "ctx"), scatter_dimension=1, tiled=True)
    qkv_new, qkv_mean, qkv_square = adam_update(
        qkv_weight, qkv_first, qkv_second, qkv_sum, rate_matrix, weight_decay
    )
    proj_new, proj_mean, proj_square = adam_update(
        proj_weight, proj_first, proj_second, proj_sum, rate_output, weight_decay
    )
    up_new, up_mean, up_square = adam_update(
        up_weight, up_first, up_second, up_sum, rate_matrix, weight_decay
    )
    down_new, down_mean, down_square = adam_update(
        down_weight, down_first, down_second, down_sum, rate_matrix, weight_decay
    )
    vectors_new, vectors_mean, vectors_square = adam_update(
        vectors, vectors_first, vectors_second, table_sum, rate_vector, 0.0
    )
    return (
        layer_out,
        token_grad,
        qkv_new,
        qkv_mean,
        qkv_square,
        proj_new,
        proj_mean,
        proj_square,
        up_new,
        up_mean,
        up_square,
        down_new,
        down_mean,
        down_square,
        vectors_new,
        vectors_mean,
        vectors_square,
    )


def solution(mesh):
    in_specs = (
        P("dp", "ctx", None),
        P("dp", "ctx", None),
        P("dp"),
        P("dp", None),
        P(("dp", "ctx"), None),
        P(("dp", "ctx"), None),
        P(("dp", "ctx"), None),
        P(("dp", "ctx"), None),
        P(("dp", "ctx"), None),
        P(("dp", "ctx"), None),
        P(("dp", "ctx"), None),
        P(("dp", "ctx"), None),
        P(("dp", "ctx"), None),
        P(("dp", "ctx"), None),
        P(("dp", "ctx"), None),
        P(("dp", "ctx"), None),
        P(None, ("dp", "ctx")),
        P(None, ("dp", "ctx")),
        P(None, ("dp", "ctx")),
    )
    out_specs = (
        P("dp", "ctx", None),
        P("dp", "ctx", None),
        P(("dp", "ctx"), None),
        P(("dp", "ctx"), None),
        P(("dp", "ctx"), None),
        P(("dp", "ctx"), None),
        P(("dp", "ctx"), None),
        P(("dp", "ctx"), None),
        P(("dp", "ctx"), None),
        P(("dp", "ctx"), None),
        P(("dp", "ctx"), None),
        P(("dp", "ctx"), None),
        P(("dp", "ctx"), None),
        P(("dp", "ctx"), None),
        P(None, ("dp", "ctx")),
        P(None, ("dp", "ctx")),
        P(None, ("dp", "ctx")),
    )
    return jax.shard_map(shards, mesh=mesh, in_specs=in_specs, out_specs=out_specs, check_vma=False)
```

```python
import jax
import jax.numpy as jnp
from jax import lax
from jax.experimental import pallas as pl
from jax.experimental.pallas import tpu as pltpu
from jax.sharding import PartitionSpec as P

HEAD_DIM = 64
STEP = 10


beta_one = 0.9
beta_two = 0.95
epsilon = 1e-08
weight_decay = 0.1
rate_matrix = 0.1
rate_output = 0.5
rate_vector = 0.4
norm_eps = 1e-05


def layer_norm(values, gain, shift):
    center = values - jnp.mean(values, -1, keepdims=True)
    variance = jnp.mean(center * center, -1, keepdims=True)
    return center * lax.rsqrt(variance + norm_eps) * gain + shift


def gelu_tanh(values):
    return (
        0.5
        * values
        * (1.0 + jnp.tanh(0.7978845608 * (values + 0.044715 * values * values * values)))
    )


def adam_update(weight, first, second, grad, rate, decay_now):
    first_new = beta_one * first + (1.0 - beta_one) * grad
    second_new = beta_two * second + (1.0 - beta_two) * grad * grad
    step_size = (
        first_new
        / (1.0 - beta_one**STEP)
        / (jnp.sqrt(second_new / (1.0 - beta_two**STEP)) + epsilon)
    )
    return (weight - rate * (step_size + decay_now * weight), first_new, second_new)


def levels():
    return lax.axis_size("dp").bit_length() - 1


def own_bit(bit):
    return (lax.axis_index("dp") // 2**bit) % 2


def swap(array, bit):
    return lax.ppermute(array, "dp", [(d, d ^ (1 << bit)) for d in range(lax.axis_size("dp"))])


def shift(array, by):
    n = lax.axis_size("ctx")
    return lax.ppermute(array, "ctx", [(c, (c + by) % n) for c in range(n)])


def pick(array, index, axis=0):
    return lax.dynamic_index_in_dim(array, index, axis, keepdims=False)


def put(array, piece, index, axis=0):
    return lax.dynamic_update_index_in_dim(array, piece, index, axis)


def to_sequence(array, order):
    n = lax.axis_size("ctx")
    me = lax.axis_index("ctx")
    out = jnp.zeros_like(array)
    out = put(out, pick(array, me), order[me])
    for by in range(1, n):
        got = shift(pick(array, (me + by) % n), by)
        out = put(out, got, order[(me - by) % n])
    return out.reshape(-1, array.shape[-1])


def from_sequence(array, order, slots):
    n = lax.axis_size("ctx")
    me = lax.axis_index("ctx")
    blocks = array.reshape(slots, -1, array.shape[-1])
    out = put(jnp.zeros_like(blocks), pick(blocks, order[me]), me)
    for by in range(1, n):
        got = shift(pick(blocks, order[(me + by) % n]), by)
        out = put(out, got, (me - by) % n)
    return out


def gather_rows(shard):
    rows, columns = shard.shape
    n = lax.axis_size("ctx")
    me = lax.axis_index("ctx")
    k = levels()
    whole = put(jnp.zeros((n, rows, columns), shard.dtype), shard, me)
    for by in range(1, n):
        whole = put(whole, shift(shard, by), (me - by) % n)
    bits = list(range(1, k))
    cut = columns // 256 * 128
    halves = []
    for order, part in ((bits, whole[:, :, :cut]), (bits[::-1], whole[:, :, cut:])):
        done = []
        for bit in order:
            axis = sum(1 for other in done if other > bit)
            got = swap(part, bit)
            done.append(bit)
            shape = part.shape[:axis] + (2,) + part.shape[axis:]
            part = put(put(jnp.zeros(shape, part.dtype), part, own_bit(bit), axis), got, 1 - own_bit(bit), axis)
        halves.append(part)
    mine = jnp.concatenate(halves, -1)
    got = swap(mine, 0)
    axis = k - 1
    shape = mine.shape[:axis] + (2,) + mine.shape[axis:]
    full = put(put(jnp.zeros(shape, mine.dtype), mine, own_bit(0), axis), got, 1 - own_bit(0), axis)
    return full.reshape(-1, columns)


def scatter_cores(whole):
    n = lax.axis_size("ctx")
    k = levels()
    rows, columns = whole.shape
    split = whole.reshape((2,) * k + (n, rows // (n * 2**k), columns))
    got = swap(pick(split, 1 - own_bit(0), k - 1), 0)
    mine = pick(split, own_bit(0), k - 1)
    return (mine.astype(jnp.float32) + got.astype(jnp.float32)).astype(jnp.bfloat16)


def scatter_planes(total):
    bits = list(range(1, levels()))
    cut = max(total.shape[-1] // 256 * 128, 128)
    ways = [(bits, total[..., :cut])]
    if total.shape[-1] > cut:
        ways.append((bits[::-1], total[..., cut:]))
    halves = []
    for order, part in ways:
        left_bits = sorted(bits, reverse=True)
        for bit in order:
            axis = left_bits.index(bit)
            got = swap(pick(part, 1 - own_bit(bit), axis), bit)
            mine = pick(part, own_bit(bit), axis)
            part = (mine.astype(jnp.float32) + got.astype(jnp.float32)).astype(jnp.bfloat16)
            left_bits.remove(bit)
        halves.append(part)
    return jnp.concatenate(halves, -1) if len(halves) > 1 else halves[0]


def scatter_last(part):
    n = lax.axis_size("ctx")
    me = lax.axis_index("ctx")
    out = pick(part, me).astype(jnp.float32)
    for by in range(1, n):
        out = out + shift(pick(part, (me + by) % n), by).astype(jnp.float32)
    return out


def product(left, right):
    return jnp.einsum("rd,re->de", left, right, preferred_element_type=jnp.float32).astype(jnp.bfloat16)


def probabilities(queries, keys, first):
    scores = lax.dot_general(
        queries, keys, (((1,), (1,)), ((), ())), preferred_element_type=jnp.float32
    ) * (HEAD_DIM ** (-0.5))
    row = lax.broadcasted_iota(jnp.int32, scores.shape, 0) + first
    column = lax.broadcasted_iota(jnp.int32, scores.shape, 1)
    scores = jnp.where(column <= row, scores, -1e30)
    expd = jnp.exp(scores - jnp.max(scores, -1, keepdims=True))
    return expd / jnp.sum(expd, -1, keepdims=True)


def attend_kernel(q_ref, k_ref, v_ref, o_ref):
    length = q_ref.shape[0]
    step = length // 2
    outs = []
    for head in range(q_ref.shape[1] // HEAD_DIM):
        lanes = slice(head * HEAD_DIM, (head + 1) * HEAD_DIM)
        parts = []
        for first in range(0, length, step):
            last = first + step
            p = probabilities(q_ref[first:last, lanes], k_ref[:last, lanes], first)
            parts.append(
                jnp.dot(p.astype(jnp.bfloat16), v_ref[:last, lanes], preferred_element_type=jnp.float32)
            )
        outs.append(jnp.concatenate(parts, 0))
    o_ref[...] = jnp.concatenate(outs, 1).astype(o_ref.dtype)


def attend_back_kernel(q_ref, k_ref, v_ref, g_ref, down_ref, up_ref, dq_ref, dk_ref, dv_ref):
    length = q_ref.shape[0]
    step = length // 2
    scale = HEAD_DIM ** (-0.5)
    all_q, all_k, all_v = [], [], []
    for head in range(q_ref.shape[1] // HEAD_DIM):
        lanes = slice(head * HEAD_DIM, (head + 1) * HEAD_DIM)
        dqs, dks, dvs = [], [], []
        for first in range(0, length, step):
            last = first + step
            q, g = q_ref[first:last, lanes], g_ref[first:last, lanes]
            k, v = k_ref[:last, lanes], v_ref[:last, lanes]
            p = probabilities(q, k, first)
            dp = lax.dot_general(g, v, (((1,), (1,)), ((), ())), preferred_element_type=jnp.float32)
            ds = (p * (dp - jnp.sum(p * dp, -1, keepdims=True))).astype(jnp.bfloat16)
            low = p.astype(jnp.bfloat16)
            dqs.append(jnp.dot(ds, k, preferred_element_type=jnp.float32) * scale)
            dks.append(
                lax.dot_general(ds, q, (((0,), (0,)), ((), ())), preferred_element_type=jnp.float32)
            )
            dvs.append(
                lax.dot_general(low, g, (((0,), (0,)), ((), ())), preferred_element_type=jnp.float32)
            )
        all_q.append(jnp.concatenate(dqs, 0))
        all_k.append(jnp.concatenate((dks[0] + dks[1][:step], dks[1][step:]), 0) * scale)
        all_v.append(jnp.concatenate((dvs[0] + dvs[1][:step], dvs[1][step:]), 0))
    dq_ref[...] = jnp.concatenate(all_q, 1).astype(dq_ref.dtype)
    dk_ref[...] = jnp.concatenate(all_k, 1).astype(dk_ref.dtype)
    dv_ref[...] = jnp.concatenate(all_v, 1).astype(dv_ref.dtype)


def attend(mixed):
    length, columns = mixed.shape
    width = columns // 3
    pairs = width // 128

    def block(which):
        return pl.BlockSpec((length, 128), lambda h: (0, which * pairs + h))

    return pl.pallas_call(
        attend_kernel,
        grid=(pairs,),
        in_specs=[block(0), block(1), block(2)],
        out_specs=block(0),
        out_shape=jax.ShapeDtypeStruct((length, width), jnp.bfloat16),
        compiler_params=pltpu.CompilerParams(vmem_limit_bytes=48 * 2**20),
        cost_estimate=pl.CostEstimate(
            flops=4 * length * length * width, bytes_accessed=8 * length * width, transcendentals=0
        ),
    )(mixed, mixed, mixed)


def attend_back(mixed, grad, down_part, up_part):
    length, columns = mixed.shape
    width = columns // 3
    pairs = width // 128

    def block(which):
        return pl.BlockSpec((length, 128), lambda h: (0, which * pairs + h))

    return pl.pallas_call(
        attend_back_kernel,
        grid=(pairs,),
        in_specs=[block(0), block(1), block(2), block(0)] + [pl.BlockSpec(memory_space=pl.ANY)] * 2,
        out_specs=[block(0)] * 3,
        out_shape=[jax.ShapeDtypeStruct((length, width), jnp.bfloat16)] * 3,
        compiler_params=pltpu.CompilerParams(vmem_limit_bytes=48 * 2**20),
        cost_estimate=pl.CostEstimate(
            flops=10 * length * length * width, bytes_accessed=14 * length * width, transcendentals=0
        ),
    )(mixed, mixed, mixed, grad, down_part, up_part)


def shards(
    tokens,
    cotangent,
    counts,
    block_order,
    qkv_weight,
    qkv_first,
    qkv_second,
    proj_weight,
    proj_first,
    proj_second,
    up_weight,
    up_first,
    up_second,
    down_weight,
    down_first,
    down_second,
    vectors,
    vectors_first,
    vectors_second,
):
    slots, span, width = tokens.shape
    ranks = lax.axis_size("ctx")
    length = span * ranks
    me = lax.axis_index("ctx")
    pad = 128
    sequence_order = lax.dynamic_index_in_dim(block_order, me, 0, keepdims=False)
    extra = vectors.T.astype(jnp.bfloat16)
    entries = extra.shape[1]
    extra = jnp.pad(extra, ((0, 0), (0, pad - entries)))
    full_qkv = gather_rows(qkv_weight.astype(jnp.bfloat16))
    table_shard = jnp.concatenate((proj_weight.astype(jnp.bfloat16), extra), 1)
    full_ext = gather_rows(table_shard)
    full_up = gather_rows(up_weight.astype(jnp.bfloat16))
    full_down = gather_rows(down_weight.astype(jnp.bfloat16))
    full_proj = full_ext[:, :width]
    table = full_ext[:, width : width + entries].T.astype(jnp.float32)
    up_bias = table[8:].reshape(-1)
    live = jnp.where(me < counts[0], 1.0, 0.0).astype(jnp.float32)
    flat = to_sequence(tokens, sequence_order).astype(jnp.float32)
    grad_out = (to_sequence(cotangent, sequence_order).astype(jnp.float32) * live).astype(jnp.bfloat16)
    normed_full, norm_pull = jax.vjp(layer_norm, flat, table[0], table[1])
    normed = normed_full.astype(jnp.bfloat16)
    bias = jnp.concatenate((table[2], jnp.zeros_like(table[2]), table[3]))
    mixed = (jnp.dot(normed, full_qkv, preferred_element_type=jnp.float32) + bias).astype(jnp.bfloat16)
    attended = attend(mixed)
    middle = flat + jnp.dot(attended, full_proj, preferred_element_type=jnp.float32) + table[4]
    normed2_full, norm2_pull = jax.vjp(layer_norm, middle, table[5], table[6])
    normed2 = normed2_full.astype(jnp.bfloat16)
    hidden = jnp.dot(normed2, full_up, preferred_element_type=jnp.float32) + up_bias
    activated, gelu_pull = jax.vjp(gelu_tanh, hidden)
    active = activated.astype(jnp.bfloat16)
    result = middle + jnp.dot(active, full_down, preferred_element_type=jnp.float32) + table[7]
    layer_out = from_sequence((result * live).astype(jnp.bfloat16), sequence_order, slots)
    down_bias_grad = jnp.sum(grad_out.astype(jnp.float32), 0)
    down_part = scatter_planes(scatter_cores(product(active, grad_out)))
    grad_active = jnp.einsum("rd,fd->rf", grad_out, full_down, preferred_element_type=jnp.float32)
    grad_hidden = gelu_pull(grad_active)[0].astype(jnp.bfloat16)
    up_bias_grad = jnp.sum(grad_hidden.astype(jnp.float32), 0)
    up_part = scatter_cores(product(normed2, grad_hidden))
    grad_normed2 = jnp.einsum("rf,df->rd", grad_hidden, full_up, preferred_element_type=jnp.float32)
    back_middle, gain2_grad, shift2_grad = norm2_pull(grad_normed2)
    grad_middle = grad_out.astype(jnp.float32) + back_middle
    grad_branch = grad_middle.astype(jnp.bfloat16)
    proj_bias_grad = jnp.sum(grad_branch.astype(jnp.float32), 0)
    proj_sum = scatter_last(scatter_planes(scatter_cores(product(attended, grad_branch))))
    grad_attended = jnp.einsum(
        "re,de->rd", grad_branch, full_proj, preferred_element_type=jnp.float32
    ).astype(jnp.bfloat16)
    grad_queries, grad_keys, grad_values = attend_back(
        mixed, grad_attended, down_part, up_part
    )
    down_sum = scatter_last(down_part)
    up_sum = scatter_last(scatter_planes(up_part))
    query_bias_grad = jnp.sum(grad_queries.astype(jnp.float32), 0)
    value_bias_grad = jnp.sum(grad_values.astype(jnp.float32), 0)
    grad_mixed = jnp.concatenate((grad_queries, grad_keys, grad_values), -1)
    qkv_sum = scatter_last(scatter_planes(scatter_cores(product(normed, grad_mixed))))
    grad_normed = jnp.einsum("re,de->rd", grad_mixed, full_qkv, preferred_element_type=jnp.float32)
    back_tokens, gain1_grad, shift1_grad = norm_pull(grad_normed)
    token_grad = from_sequence(
        (grad_middle + back_tokens).astype(jnp.bfloat16), sequence_order, slots
    ).astype(jnp.float32)
    small_grads = jnp.stack(
        (
            gain1_grad,
            shift1_grad,
            query_bias_grad,
            value_bias_grad,
            proj_bias_grad,
            gain2_grad,
            shift2_grad,
            down_bias_grad,
        )
    )
    table_grad = jnp.concatenate((small_grads, up_bias_grad.reshape(-1, width)), 0)
    table_rows = jnp.pad(table_grad.T.astype(jnp.bfloat16), ((0, 0), (0, pad - entries)))
    table_sum = scatter_last(scatter_planes(scatter_cores(table_rows)))[:, :entries].T
    qkv_new, qkv_mean, qkv_square = adam_update(
        qkv_weight, qkv_first, qkv_second, qkv_sum, rate_matrix, weight_decay
    )
    proj_new, proj_mean, proj_square = adam_update(
        proj_weight, proj_first, proj_second, proj_sum, rate_output, weight_decay
    )
    up_new, up_mean, up_square = adam_update(
        up_weight, up_first, up_second, up_sum, rate_matrix, weight_decay
    )
    down_new, down_mean, down_square = adam_update(
        down_weight, down_first, down_second, down_sum, rate_matrix, weight_decay
    )
    vectors_new, vectors_mean, vectors_square = adam_update(
        vectors, vectors_first, vectors_second, table_sum, rate_vector, 0.0
    )
    return (
        layer_out,
        token_grad,
        qkv_new,
        qkv_mean,
        qkv_square,
        proj_new,
        proj_mean,
        proj_square,
        up_new,
        up_mean,
        up_square,
        down_new,
        down_mean,
        down_square,
        vectors_new,
        vectors_mean,
        vectors_square,
    )


def solution(mesh):
    in_specs = (
        P("dp", "ctx", None),
        P("dp", "ctx", None),
        P("dp"),
        P("dp", None),
        P(("dp", "ctx"), None),
        P(("dp", "ctx"), None),
        P(("dp", "ctx"), None),
        P(("dp", "ctx"), None),
        P(("dp", "ctx"), None),
        P(("dp", "ctx"), None),
        P(("dp", "ctx"), None),
        P(("dp", "ctx"), None),
        P(("dp", "ctx"), None),
        P(("dp", "ctx"), None),
        P(("dp", "ctx"), None),
        P(("dp", "ctx"), None),
        P(None, ("dp", "ctx")),
        P(None, ("dp", "ctx")),
        P(None, ("dp", "ctx")),
    )
    out_specs = (
        P("dp", "ctx", None),
        P("dp", "ctx", None),
        P(("dp", "ctx"), None),
        P(("dp", "ctx"), None),
        P(("dp", "ctx"), None),
        P(("dp", "ctx"), None),
        P(("dp", "ctx"), None),
        P(("dp", "ctx"), None),
        P(("dp", "ctx"), None),
        P(("dp", "ctx"), None),
        P(("dp", "ctx"), None),
        P(("dp", "ctx"), None),
        P(("dp", "ctx"), None),
        P(("dp", "ctx"), None),
        P(None, ("dp", "ctx")),
        P(None, ("dp", "ctx")),
        P(None, ("dp", "ctx")),
    )
    return jax.shard_map(shards, mesh=mesh, in_specs=in_specs, out_specs=out_specs, check_vma=False)
```
